32 devices in a mesh: section: 2 (over core), vocab: 16 (over z, y, x).
Axes of the slice: x: 2, y: 2, z: 4, core: 2. Of those that a mesh axis runs over, the one named last changes fastest.
Arguments:
- hidden: bfloat16 [2, 512, 8192], P('section', None, 'vocab'), may hold values from -160 to 160
- final_hidden: bfloat16 [512, 8192], P('section', 'vocab'), may hold values from -160 to 160
- row_pick: int32 [2, 128], P('section'), may hold values from 0 to 511
- trans_weight: bfloat16 [2, 8192, 8192], P('section', None, 'vocab'), may hold values from -0.0625 to 0.0625
- trans_bias: bfloat16 [2, 8192], P('section', 'vocab'), may hold values from -6 to 6
- norm_gain: bfloat16 [8192], P('vocab'), may hold values from 0.5 to 1.5
- unembed: bfloat16 [8192, 8192], P('section', 'vocab'), may hold values from -100 to 100
Outputs:
- grad_weight: bfloat16 [2, 8192, 8192], P('section', None, 'vocab')
- grad_bias: float32 [2, 8192], P('section', 'vocab')
- kl_mean: float32 [2], P('section')
The draws below stay inside these ranges and needn't reach their ends.
All inputs are finite; a program needn't handle non-finite values.
Results may differ from the reference program's by a relative error of at most 0.024.
Values may be sent and summed in bfloat16 or wider, within the bound.
No kernel may reach another device: no remote copies, remote signals or barrier semaphores. Data moves between devices by JAX's collectives and lax.ppermute only.
A program may use at most 64 MiB of HBM per device.

```python
import math
import jax
import jax.numpy as jnp
from jax import lax

D = 8192
ROWS = 128
POOL = 512
VOCAB = 8192
LAYERS = 2


def scaled_field(key, shape):
    base_key, row_key, column_key = jax.random.split(key, 3)
    columns = jnp.exp(jax.random.uniform(column_key, (shape[-1],), jnp.float32, -1.15, 1.15))
    scales = jnp.exp(jax.random.uniform(row_key, shape[:-1] + (1,), jnp.float32, 0.0, 2.3))
    values = jnp.clip(jax.random.normal(base_key, shape, jnp.float32), -5.0, 5.0)
    return jnp.clip(values * columns * scales, -160.0, 160.0).astype(jnp.bfloat16)


def draw_hidden(key, part):
    return scaled_field(jax.random.fold_in(key, 11), (LAYERS, POOL, D))


def draw_final_hidden(key, part):
    return scaled_field(jax.random.fold_in(key, 23), (POOL, D))


def draw_unembed(key, part):
    base_key = jax.random.fold_in(jax.random.fold_in(key, 37), 0)
    spread = 3.0 / math.sqrt(D)
    table = jnp.clip(jax.random.normal(base_key, (D, VOCAB), jnp.float32), -6.0, 6.0) * spread
    return jnp.clip(table, -100.0, 100.0).astype(jnp.bfloat16)


def set_ends(array, stream_key, smallest, top_value):
    extent = array.shape
    spot = [jax.random.randint(jax.random.fold_in(stream_key, axis), (), 0, extent[axis]) for axis in range(len(extent))]
    array = array.at[tuple(spot)].set(smallest)
    longest = extent.index(max(extent))
    spot[longest] = (spot[longest] + 1) % extent[longest]
    return array.at[tuple(spot)].set(top_value)


def level_of(rng, dims, cuts, least, top_value):
    gain, own = 1.0, jax.random.fold_in(rng, 6)
    for position, blocks in cuts:
        steps = jnp.exp(jax.random.uniform(jax.random.fold_in(own, position), (blocks,), jnp.float32, least / len(cuts), top_value / len(cuts)))
        gain = gain * jnp.repeat(steps, dims[position] // blocks).reshape([-1 if axis == position else 1 for axis in range(len(dims))])
    return gain


def gaussian(own_key, extent, width, limit, cuts=(), dtype=jnp.bfloat16):
    array = jax.random.normal(own_key, extent, jnp.float32) * width
    if len(cuts) > 0:
        array = level_of(own_key, extent, cuts, -0.22, 0.18) * array
    return jnp.clip(array, min=-limit, max=limit).astype(dtype)


def setup_inputs(seed: int = 0) -> dict:
    seeds = jax.random.split(jax.random.key(seed), 8)
    hidden = draw_hidden(jax.random.fold_in(seeds[7], 71), 0)
    final_hidden = draw_final_hidden(jax.random.fold_in(seeds[7], 71), 0)
    row_pick = set_ends(jax.random.randint(seeds[2], (LAYERS, ROWS), 0, POOL), jax.random.fold_in(seeds[2], 1), 0, POOL - 1).astype(jnp.int32)
    trans_weight = gaussian(seeds[3], (LAYERS, D, D), D ** -0.5, 0.0625, ((0, 2), (2, 16)))
    trans_bias = gaussian(seeds[4], (LAYERS, D), 1.0, 6.0, ((0, 2), (1, 16)))
    norm_gain = jnp.clip(1.0 + 0.1 * jax.random.normal(seeds[5], (D,), jnp.float32), 0.5, 1.5).astype(jnp.bfloat16)
    unembed = draw_unembed(jax.random.fold_in(seeds[7], 71), 0)
    return dict(hidden=hidden, final_hidden=final_hidden, row_pick=row_pick, trans_weight=trans_weight, trans_bias=trans_bias, norm_gain=norm_gain, unembed=unembed)


epsilon = 1e-05

def log_softmax_rows(values):
    highest = lax.optimization_barrier(jnp.max(values, axis=-1, keepdims=True))
    shifted = values - highest
    return shifted - jnp.log(lax.optimization_barrier(jnp.sum(jnp.exp(shifted), axis=-1, keepdims=True)))

def reference(hidden, final_hidden, row_pick, trans_weight, trans_bias, norm_gain, unembed):
    gain_cols = norm_gain.astype(jnp.float32)
    grad_weights = []
    grad_biases = []
    kl_values = []
    for index_layer in range(LAYERS):
        picked = row_pick[index_layer]
        inputs = hidden[index_layer][picked]
        finals = final_hidden[picked].astype(jnp.float32)
        trans = inputs.astype(jnp.float32) + jnp.dot(inputs, trans_weight[index_layer], preferred_element_type=jnp.float32) + trans_bias[index_layer].astype(jnp.float32)
        trans_scale = lax.rsqrt(lax.optimization_barrier(jnp.mean(trans * trans, axis=-1)) + epsilon)
        final_scale = lax.rsqrt(lax.optimization_barrier(jnp.mean(finals * finals, axis=-1)) + epsilon)
        normed = (trans * trans_scale[:, None] * gain_cols).astype(jnp.bfloat16)
        target = (finals * final_scale[:, None] * gain_cols).astype(jnp.bfloat16)
        log_trans = log_softmax_rows(jnp.dot(normed, unembed, preferred_element_type=jnp.float32))
        log_target = log_softmax_rows(jnp.dot(target, unembed, preferred_element_type=jnp.float32))
        probs = jnp.exp(log_target)
        kl_values.append(jnp.mean(lax.optimization_barrier(jnp.sum(probs * (log_target - log_trans), axis=-1))))
        dlogits = (jnp.exp(log_trans) - probs).astype(jnp.bfloat16)
        dnormed = jnp.dot(dlogits, unembed.T, preferred_element_type=jnp.float32)
        scaled = dnormed * gain_cols
        product = lax.optimization_barrier(jnp.mean(scaled * trans, axis=-1))
        dtrans = trans_scale[:, None] * (scaled - trans * (trans_scale * trans_scale * product)[:, None])
        grad_weights.append(jnp.dot(inputs.T, dtrans.astype(jnp.bfloat16), preferred_element_type=jnp.float32).astype(jnp.bfloat16))
        grad_biases.append(lax.optimization_barrier(jnp.sum(dtrans, axis=0)))
    return (jnp.stack(grad_weights), jnp.stack(grad_biases), jnp.stack(kl_values))
```

```python
import jax
import jax.numpy as jnp
from jax import lax
from jax.sharding import PartitionSpec as P

epsilon = 1e-05
f32 = jnp.float32
bf16 = jnp.bfloat16


def swap(value, offset, count):
    return lax.ppermute(value, "vocab", [(i, i ^ offset) for i in range(count)])


def gather_pieces(own, count):
    pieces = {0: own}
    outer = range(4, count, 4)
    for k in outer:
        pieces[k] = swap(own, k, count)
    for number, base in enumerate(range(0, count, 4)):
        pieces[base + 1] = swap(pieces[base], 1, count)
        pieces[base + 2] = swap(pieces[base], 2, count)
        if number % 2:
            pieces[base + 3] = swap(pieces[base + 2], 1, count)
        else:
            pieces[base + 3] = swap(pieces[base + 1], 2, count)
    return pieces


def arrival_order(count):
    order = [0, 4, 1, 2, 5, 6, 3, 7] if count > 4 else [0, 1, 2, 3]
    for base in range(8, count, 8):
        order += [base, base + 4, base + 1, base + 2, base + 5, base + 6, base + 3, base + 7]
    return order


def total(*parts):
    result = parts[0].astype(f32)
    for part in parts[1:]:
        result = result + part.astype(f32)
    return result


def scatter_sum(block_of, count):
    bases = list(range(0, count, 4))[::-1]
    blocks = {}
    for base in bases:
        far = block_of(base + 3)
        if (base // 4) % 2:
            blocks[base + 1] = block_of(base + 1)
            blocks[base + 2] = total(block_of(base + 2), swap(far, 1, count)).astype(bf16)
        else:
            blocks[base + 2] = block_of(base + 2)
            blocks[base + 1] = total(block_of(base + 1), swap(far, 2, count)).astype(bf16)
    result = None
    for base in bases:
        near = total(block_of(base), swap(blocks[base + 1], 1, count), swap(blocks[base + 2], 2, count))
        if base:
            near = swap(near.astype(bf16), base, count)
        result = near if result is None else total(result, near)
    return result


def split_words(value):
    high = lax.reduce_precision(value, 8, 7)
    rest = value - high
    middle = lax.reduce_precision(rest, 8, 7)
    return jnp.stack([high, middle, rest - middle]).astype(bf16)


def with_squares(rows, squares):
    words = split_words(squares)
    extra = jnp.zeros((8, rows.shape[1]), bf16).at[:3, : squares.shape[0]].set(words)
    return jnp.concatenate([rows, extra], axis=0)


def squares_of(pieces, row_count):
    return sum(jnp.sum(piece[row_count : row_count + 3, :row_count].astype(f32), axis=0) for piece in pieces)


def gather_stats(stats, count):
    parts = jnp.stack([stats] + [swap(stats, k, count) for k in range(4, count, 4)])
    return jnp.concatenate([parts] + [swap(parts, k, count) for k in (1, 2, 3)])


def per_device(hidden, final_hidden, row_pick, trans_weight, trans_bias, norm_gain, unembed):
    count = lax.axis_size("vocab")
    sections = lax.axis_size("section")
    me = lax.axis_index("vocab")
    section = lax.axis_index("section")
    gain = norm_gain.astype(f32)
    width = trans_weight.shape[1]
    cols = trans_weight.shape[2]
    row_count = row_pick.shape[1]
    picked = row_pick[0]

    own_inputs = hidden[0][picked]
    inputs = gather_pieces(own_inputs, count)

    unembed_all = jnp.concatenate(
        [unembed]
        + [
            lax.ppermute(unembed, "section", [((i + k) % sections, i) for i in range(sections)])
            for k in range(1, sections)
        ],
        axis=0,
    )

    def unembed_block(index):
        start = lax.rem(index * cols + width - section * unembed.shape[0], width)
        return lax.dynamic_slice_in_dim(unembed_all, start, cols, axis=0)

    final_all = lax.all_gather(final_hidden, "section", axis=0, tiled=True)
    finals = final_all[picked].astype(f32)
    target_own = with_squares((finals * gain).astype(bf16), jnp.sum(finals * finals, axis=-1))
    targets = lax.all_gather(target_own, "vocab", axis=0)

    trans = own_inputs.astype(f32) + trans_bias[0].astype(f32)
    for k in arrival_order(count):
        weight = lax.dynamic_slice_in_dim(trans_weight[0], (me ^ k) * cols, cols, axis=0)
        trans = trans + jnp.dot(inputs[k], weight, preferred_element_type=f32)
    trans_own = with_squares((trans * gain).astype(bf16), jnp.sum(trans * trans, axis=-1))
    normed = gather_pieces(trans_own, count)

    target_logits = 0.0
    for k in range(count):
        target_logits = target_logits + jnp.dot(targets[k], unembed_block(k), preferred_element_type=f32)
    final_squares = squares_of([targets[k] for k in range(count)], row_count)
    final_scale = lax.rsqrt(final_squares / width + epsilon)
    target_logits = target_logits[:row_count] * final_scale[:, None]

    logits = 0.0
    for k in arrival_order(count):
        logits = logits + jnp.dot(normed[k], unembed_block(me ^ k), preferred_element_type=f32)
    trans_squares = squares_of([normed[k] for k in range(count)], row_count)
    trans_scale = lax.rsqrt(trans_squares / width + epsilon)
    logits = logits[:row_count] * trans_scale[:, None]

    trans_max = jnp.max(logits, axis=-1)
    target_max = jnp.max(target_logits, axis=-1)
    shifted = logits - trans_max[:, None]
    trans_exp = jnp.exp(shifted)
    target_exp = jnp.exp(target_logits - target_max[:, None])
    stats = jnp.stack(
        [
            trans_max,
            jnp.sum(trans_exp, axis=-1),
            jnp.sum(trans_exp * shifted, axis=-1),
            target_max,
            jnp.sum(target_exp, axis=-1),
            jnp.sum(target_exp * (target_logits - logits), axis=-1),
            jnp.sum(target_exp * shifted, axis=-1),
            jnp.zeros_like(trans_max),
        ]
    )
    every = gather_stats(stats, count)
    top = jnp.max(every[:, 0], axis=0)
    target_top = jnp.max(every[:, 3], axis=0)
    drop = every[:, 0] - top
    factor = jnp.exp(drop)
    target_factor = jnp.exp(every[:, 3] - target_top)
    trans_sum = jnp.sum(factor * every[:, 1], axis=0)
    target_sum = jnp.sum(target_factor * every[:, 4], axis=0)
    log_sum = top + jnp.log(trans_sum)
    target_log_sum = target_top + jnp.log(target_sum)
    kl_rows = jnp.sum(target_factor * every[:, 5], axis=0) / target_sum - (target_log_sum - log_sum)
    logit_dots = (
        jnp.sum(factor * (every[:, 2] + every[:, 1] * drop), axis=0) / trans_sum
        - jnp.sum(target_factor * (every[:, 6] + every[:, 4] * drop), axis=0) / target_sum
    )

    dlogits = (
        jnp.exp(logits - log_sum[:, None]) - jnp.exp(target_logits - target_log_sum[:, None])
    ).astype(bf16)

    def dnormed_block(k):
        return lax.dot_general(
            dlogits, unembed_block(me ^ k), (((1,), (1,)), ((), ())), preferred_element_type=f32
        ).astype(bf16)

    dnormed = scatter_sum(dnormed_block, count)
    product = logit_dots / (width * trans_scale)
    dtrans = trans_scale[:, None] * (
        dnormed * gain - trans * (trans_scale * trans_scale * product)[:, None]
    )

    inputs_all = jnp.zeros((row_count, width), bf16)
    for k in arrival_order(count):
        inputs_all = lax.dynamic_update_slice_in_dim(inputs_all, inputs[k], (me ^ k) * cols, axis=1)
    grad_weight = lax.dot_general(
        inputs_all, dtrans.astype(bf16), (((0,), (0,)), ((), ())), preferred_element_type=f32
    ).astype(bf16)
    grad_bias = jnp.sum(dtrans, axis=0)
    kl_mean = jnp.sum(kl_rows) / row_count
    return grad_weight[None], grad_bias[None], kl_mean[None]


def solution(mesh):
    placed = (
        P("section", None, "vocab"),
        P("section", "vocab"),
        P("section", None),
        P("section", None, "vocab"),
        P("section", "vocab"),
        P("vocab"),
        P("section", "vocab"),
    )
    return jax.shard_map(
        per_device,
        mesh=mesh,
        in_specs=placed,
        out_specs=(P("section", None, "vocab"), P("section", "vocab"), P("section")),
        check_vma=False,
    )
```

```python
import functools

import jax
import jax.numpy as jnp
from jax import lax
from jax.experimental import pallas as pl
from jax.experimental.pallas import tpu as pltpu
from jax.sharding import PartitionSpec as P

epsilon = 1e-05
f32 = jnp.float32
bf16 = jnp.bfloat16
words_height = 16
vmem = pl.BlockSpec(memory_space=pltpu.VMEM)
smem = pl.BlockSpec(memory_space=pltpu.SMEM)
anywhere = pl.BlockSpec(memory_space=pl.ANY)


def kernel_call(body, name, in_specs, out_shapes, out_specs, scratch, flops, moved):
    return pl.pallas_call(
        body,
        name=name,
        in_specs=in_specs,
        out_shape=out_shapes,
        out_specs=out_specs,
        scratch_shapes=scratch,
        cost_estimate=pl.CostEstimate(flops=flops, bytes_accessed=moved, transcendentals=0),
        compiler_params=pltpu.CompilerParams(vmem_limit_bytes=32 * 1024 * 1024),
    )


def swap(value, offset, count):
    return lax.ppermute(value, "vocab", [(i, i ^ offset) for i in range(count)])


def gather_pieces(own, count):
    pieces = {0: own}
    for k in range(4, count, 4):
        pieces[k] = swap(own, k, count)
    for number, base in enumerate(range(0, count, 4)):
        pieces[base + 1] = swap(pieces[base], 1, count)
        pieces[base + 2] = swap(pieces[base], 2, count)
        if number % 2:
            pieces[base + 3] = swap(pieces[base + 2], 1, count)
        else:
            pieces[base + 3] = swap(pieces[base + 1], 2, count)
    return pieces


def total(*parts):
    result = parts[0].astype(f32)
    for part in parts[1:]:
        result = result + part.astype(f32)
    return result


def scatter_sums(blocks, count):
    bases = list(range(0, count, 4))[::-1]
    second = {}
    for base in bases:
        if (base // 4) % 2:
            second[base + 1] = blocks[base + 1]
            second[base + 2] = total(blocks[base + 2], swap(blocks[base + 3], 1, count)).astype(bf16)
        else:
            second[base + 2] = blocks[base + 2]
            second[base + 1] = total(blocks[base + 1], swap(blocks[base + 3], 2, count)).astype(bf16)
    terms = []
    for base in bases:
        near = swap(second[base + 1], 1, count), swap(second[base + 2], 2, count)
        if base:
            terms.append(swap(total(blocks[base], *near).astype(bf16), base, count))
        else:
            terms.extend((blocks[0], *near))
    return terms


def pull(place, k, tables, buffer, sem):
    height = buffer.shape[0]
    index = place[0] ^ k
    if len(tables) == 1:
        rows = pl.ds(pl.multiple_of(index * height, height), height)
        pltpu.make_async_copy(tables[0].at[rows], buffer, sem).start()
        return
    per_table = tables[0].shape[0] // height
    rows = pl.ds(pl.multiple_of(lax.rem(index, per_table) * height, height), height)
    turn = lax.rem(lax.div(index, per_table) - place[1] + len(tables), len(tables))
    for number, table in enumerate(tables):

        @pl.when(turn == number)
        def _():
            pltpu.make_async_copy(table.at[rows], buffer, sem).start()


def arrived(tables, buffer, sem):
    pltpu.make_async_copy(tables[0].at[pl.ds(0, buffer.shape[0])], buffer, sem).wait()


def as_row(column):
    size = column.shape[0]
    return jnp.transpose(jnp.broadcast_to(column, (size, size)))[:1]


def as_column(row):
    size = row.shape[1]
    return jnp.transpose(jnp.broadcast_to(row, (size, size)))[:, :1]


def words_of(row, first):
    high = row.astype(bf16).astype(f32)
    middle = (row - high).astype(bf16).astype(f32)
    low = row - high - middle
    line = lax.broadcasted_iota(jnp.int32, (words_height, row.shape[1]), 0)
    block = jnp.where(line == first, high, 0.0)
    block = jnp.where(line == first + 1, middle, block)
    return jnp.where(line == first + 2, low, block)


def head_kernel(inputs, finals, gain, first, tail):
    rows = inputs.shape[0]
    half = rows // 2
    value = finals[...].astype(f32)
    target = (value * gain[...]).astype(bf16)
    first[:rows] = inputs[...]
    first[rows:] = target[:half]
    tail[:half] = target[half:]
    tail[half:] = jnp.zeros((words_height, value.shape[1]), bf16)
    squares = as_row(jnp.sum(value * value, axis=1, keepdims=True))
    tail[half:, :rows] = words_of(squares, 3).astype(bf16)


def contract_kernel(order, lines, table_count, words, place, *refs):
    pieces, refs = refs[: len(order)], refs[len(order) :]
    tables, refs = refs[:table_count], refs[table_count:]
    result, refs = refs[0], refs[1:]
    if words:
        word_sum, refs = refs[0], refs[1:]
    buffer, sems = refs
    for slot, k in enumerate(order):
        pull(place, k, tables, buffer.at[slot], sems.at[slot])
    for slot in range(len(order)):
        arrived(tables, buffer.at[slot], sems.at[slot])
        part = jnp.dot(pieces[slot][lines[0] : lines[1]], buffer[slot], preferred_element_type=f32)
        if slot:
            result[...] += part
        else:
            result[...] = part
    if words:
        word_sum[...] = sum(piece[-words_height:].astype(f32) for piece in pieces)


def trans_kernel(order, place, *refs):
    pieces, refs = refs[: len(order)], refs[len(order) :]
    weight, so_far, own, bias, gain, tail, trans, payload, buffer, sems = refs
    rows = so_far.shape[0]
    for slot, k in enumerate(order):
        pull(place, k, [weight], buffer.at[slot], sems.at[slot])
    trans[...] = so_far[...] + own[:rows].astype(f32) + bias[...]
    for slot in range(len(order)):
        arrived([weight], buffer.at[slot], sems.at[slot])
        trans[...] += jnp.dot(pieces[slot][:rows], buffer[slot], preferred_element_type=f32)
    value = trans[...]
    payload[:rows] = (value * gain[...]).astype(bf16)
    payload[rows:] = tail[...]
    squares = as_row(jnp.sum(value * value, axis=1, keepdims=True))
    start = payload.shape[0] - words_height
    payload[start:, :rows] = (
        words_of(squares, 0) + tail[-words_height:, :rows].astype(f32)
    ).astype(bf16)


def logits_kernel(order, table_count, width, place, *refs):
    pieces, refs = refs[: len(order)], refs[len(order) :]
    tables, refs = refs[:table_count], refs[table_count:]
    so_far, early_words, target_half, logits, target_logits, stats, scale, buffer, sems, acc = refs
    rows = logits.shape[0]
    half = target_half.shape[0]
    for slot, k in enumerate(order):
        pull(place, k, tables, buffer.at[slot], sems.at[slot])
    acc[...] = so_far[...]
    words = early_words[...] + sum(piece[-words_height:].astype(f32) for piece in pieces)
    words = words[:, :rows]
    trans_scale = lax.rsqrt((words[0:1] + words[1:2] + words[2:3]) / width + epsilon)
    final_scale = lax.rsqrt((words[3:4] + words[4:5] + words[5:6]) / width + epsilon)
    scale[...] = jnp.broadcast_to(trans_scale, scale.shape)
    trans_column, final_column = as_column(trans_scale), as_column(final_scale)
    for slot in range(len(order)):
        arrived(tables, buffer.at[slot], sems.at[slot])
        acc[...] += jnp.dot(pieces[slot][...], buffer[slot], preferred_element_type=f32)
    trans_logits = acc[:rows] * trans_column
    logits[...] = trans_logits
    target_logits[:half] = target_half[...] * final_column[:half]
    target_logits[half:] = acc[rows : rows + rows - half] * final_column[half:]
    target = target_logits[...]
    trans_max = jnp.max(trans_logits, axis=1, keepdims=True)
    target_max = jnp.max(target, axis=1, keepdims=True)
    shifted = trans_logits - trans_max
    trans_exp = jnp.exp(shifted)
    target_exp = jnp.exp(target - target_max)
    columns = (
        trans_max,
        jnp.sum(trans_exp, axis=1, keepdims=True),
        jnp.sum(trans_exp * shifted, axis=1, keepdims=True),
        target_max,
        jnp.sum(target_exp, axis=1, keepdims=True),
        jnp.sum(target_exp * (target - trans_logits), axis=1, keepdims=True),
        jnp.sum(target_exp * shifted, axis=1, keepdims=True),
    )
    lane = lax.broadcasted_iota(jnp.int32, (rows, rows), 1)
    packed = jnp.zeros((rows, rows), f32)
    for number, column in enumerate(columns):
        packed = jnp.where(lane == number, column, packed)
    stats[...] = jnp.transpose(packed)[: stats.shape[0]]


def backward_blocks(order, place, tables, dlogits, outs, buffer, sems):
    for slot in range(len(order)):
        arrived(tables, buffer.at[slot], sems.at[slot])
        outs[slot][...] = lax.dot_general(
            dlogits, buffer[slot], (((1,), (1,)), ((), ())), preferred_element_type=f32
        ).astype(bf16)


def first_backward_kernel(order, table_count, place, *refs):
    tables, refs = refs[:table_count], refs[table_count:]
    logits, target_logits, *stats = refs[:6]
    refs = refs[6:]
    dlogits, info, *outs = refs[:-2]
    buffer, sems = refs[-2:]
    for slot, k in enumerate(order):
        pull(place, k, tables, buffer.at[slot], sems.at[slot])
    every = [part[i] for part in stats for i in range(part.shape[0])]
    top = functools.reduce(jnp.maximum, [s[0:1] for s in every])
    target_top = functools.reduce(jnp.maximum, [s[3:4] for s in every])
    trans_sum = target_sum = kl_sum = trans_dot = target_dot = 0.0
    for s in every:
        drop = s[0:1] - top
        factor = jnp.exp(drop)
        target_factor = jnp.exp(s[3:4] - target_top)
        trans_sum += factor * s[1:2]
        target_sum += target_factor * s[4:5]
        kl_sum += target_factor * s[5:6]
        trans_dot += factor * (s[2:3] + s[1:2] * drop)
        target_dot += target_factor * (s[6:7] + s[4:5] * drop)
    log_sum = top + jnp.log(trans_sum)
    target_log_sum = target_top + jnp.log(target_sum)
    value = (
        jnp.exp(logits[...] - as_column(log_sum))
        - jnp.exp(target_logits[...] - as_column(target_log_sum))
    ).astype(bf16)
    dlogits[...] = value
    line = lax.broadcasted_iota(jnp.int32, info.shape, 0)
    kl_rows = kl_sum / target_sum - (target_log_sum - log_sum)
    info[...] = jnp.where(line == 0, kl_rows, trans_dot / trans_sum - target_dot / target_sum)
    backward_blocks(order, place, tables, value, outs, buffer, sems)


def later_backward_kernel(order, table_count, place, *refs):
    tables, refs = refs[:table_count], refs[table_count:]
    dlogits, *outs = refs[:-2]
    buffer, sems = refs[-2:]
    for slot, k in enumerate(order):
        pull(place, k, tables, buffer.at[slot], sems.at[slot])
    backward_blocks(order, place, tables, dlogits[...], outs, buffer, sems)


def weight_kernel(count, term_count, width, place, *refs):
    pieces, refs = refs[:count], refs[count:]
    terms, refs = refs[:term_count], refs[term_count:]
    trans, gain, scale, info, grad_weight, grad_bias, kl, buffer, sems = refs
    rows = trans.shape[0]
    height = buffer.shape[1]
    dnormed = functools.reduce(lambda a, b: a + b, [term[...].astype(f32) for term in terms])
    scale_row = scale[0:1]
    weight_row = scale_row * scale_row * info[1:2] / (width * scale_row)
    dtrans = as_column(scale_row) * (dnormed * gain[...] - trans[...] * as_column(weight_row))
    grad_bias[...] = jnp.sum(dtrans, axis=0, keepdims=True)
    kl[...] = jnp.broadcast_to(jnp.sum(info[0:1], axis=1, keepdims=True) / rows, kl.shape)
    rounded = dtrans.astype(bf16)
    copies = []
    for k in range(count):
        buffer[k] = lax.dot_general(
            pieces[k][:rows], rounded, (((0,), (0,)), ((), ())), preferred_element_type=f32
        ).astype(bf16)
        start = pl.multiple_of((place[0] ^ k) * height, height)
        copies.append(pltpu.make_async_copy(buffer.at[k], grad_weight.at[0, pl.ds(start, height)], sems.at[k]))
        copies[-1].start()
    for copy in copies:
        copy.wait()


def per_device(hidden, final_hidden, row_pick, trans_weight, trans_bias, norm_gain, unembed):
    count = lax.axis_size("vocab")
    sections = lax.axis_size("section")
    me = lax.axis_index("vocab")
    section = lax.axis_index("section")
    place = jnp.stack([me, section]).astype(jnp.int32)
    width, cols = trans_weight.shape[1:]
    rows = row_pick.shape[1]
    half = rows // 2
    picked = row_pick[0]
    weight = trans_weight[0]
    gain = norm_gain.astype(f32)[None]
    bias = trans_bias.astype(f32)
    shape = jax.ShapeDtypeStruct
    entries = unembed.shape[1]
    weight_block = 2 * cols * cols
    table_block = 2 * cols * entries

    def table_scratch(number, columns):
        return [pltpu.VMEM((number, cols, columns), bf16), pltpu.SemaphoreType.DMA((number,))]

    final_all = lax.all_gather(final_hidden, "section", axis=0, tiled=True)
    first_own, tail = kernel_call(
        head_kernel,
        "head",
        [vmem] * 3,
        (shape((rows + half, cols), bf16), shape((rows - half + words_height, cols), bf16)),
        (vmem, vmem),
        [],
        0,
        6 * rows * cols,
    )(hidden[0][picked], final_all[picked], gain)
    first = gather_pieces(first_own, count)

    tables = [unembed] + [
        lax.ppermute(unembed, "section", [((i + k) % sections, i) for i in range(sections)])
        for k in range(1, sections)
    ]

    early = list(range(count // 2))
    late = list(range(count // 2, count))
    side = len(early)
    so_far = kernel_call(
        functools.partial(contract_kernel, early, (0, rows), 1, False),
        "trans_early",
        [smem] + [vmem] * side + [anywhere],
        shape((rows, cols), f32),
        vmem,
        table_scratch(side, cols),
        side * rows * weight_block,
        side * weight_block,
    )(place, *[first[k] for k in early], weight)
    payload_shape = shape((first_own.shape[0] + words_height, cols), bf16)
    trans, second_own = kernel_call(
        functools.partial(trans_kernel, late),
        "trans_late",
        [smem] + [vmem] * side + [anywhere] + [vmem] * 5,
        (shape((rows, cols), f32), payload_shape),
        (vmem, vmem),
        table_scratch(side, cols),
        side * rows * weight_block,
        side * weight_block,
    )(place, *[first[k] for k in late], weight, so_far, first_own, bias, gain, tail)
    second = gather_pieces(second_own, count)

    every = early + late
    target_half = kernel_call(
        functools.partial(contract_kernel, every, (rows, rows + half), sections, False),
        "target_half",
        [smem] + [vmem] * count + [anywhere] * sections,
        shape((half, entries), f32),
        vmem,
        table_scratch(count, entries),
        count * half * table_block,
        count * table_block,
    )(place, *[first[k] for k in every], *tables)
    height = payload_shape.shape[0]
    so_far, words = kernel_call(
        functools.partial(contract_kernel, early, (0, height), sections, True),
        "logits_early",
        [smem] + [vmem] * side + [anywhere] * sections,
        (shape((height, entries), f32), shape((words_height, cols), f32)),
        (vmem, vmem),
        table_scratch(side, entries),
        side * height * table_block,
        side * table_block,
    )(place, *[second[k] for k in early], *tables)
    logits, target_logits, stats, scale = kernel_call(
        functools.partial(logits_kernel, late, sections, width),
        "logits_late",
        [smem] + [vmem] * side + [anywhere] * sections + [vmem] * 3,
        (shape((rows, entries), f32), shape((rows, entries), f32), shape((8, rows), f32), shape((8, rows), f32)),
        (vmem,) * 4,
        table_scratch(side, entries) + [pltpu.VMEM((height, entries), f32)],
        side * height * table_block,
        side * table_block,
    )(place, *[second[k] for k in late], *tables, so_far, words, target_half)

    line_stats = jnp.stack([stats] + [swap(stats, k, count) for k in range(4, count, 4)])
    all_stats = [line_stats] + [swap(line_stats, k, count) for k in (1, 2, 3)]

    blocks = {}
    far = [base + 3 for base in range(0, count, 4)][::-1]
    piece = shape((rows, cols), bf16)
    dlogits, info, *made = kernel_call(
        functools.partial(first_backward_kernel, far, sections),
        "backward_far",
        [smem] + [anywhere] * sections + [vmem] * 6,
        (shape((rows, entries), bf16), shape((8, rows), f32), *[piece] * len(far)),
        (vmem,) * (2 + len(far)),
        table_scratch(len(far), entries),
        len(far) * rows * table_block,
        len(far) * table_block,
    )(place, *tables, logits, target_logits, *all_stats)
    blocks.update(zip(far, made))
    rest = [base + k for k in (1, 2, 0) for base in range(0, count, 4)[::-1]]
    made = kernel_call(
        functools.partial(later_backward_kernel, rest, sections),
        "backward_rest",
        [smem] + [anywhere] * sections + [vmem],
        tuple([piece] * len(rest)),
        (vmem,) * len(rest),
        table_scratch(len(rest), entries),
        len(rest) * rows * table_block,
        len(rest) * table_block,
    )(place, *tables, dlogits)
    blocks.update(zip(rest, made))
    terms = scatter_sums(blocks, count)

    grad_weight, grad_bias, kl = kernel_call(
        functools.partial(weight_kernel, count, len(terms), width),
        "grad_weight",
        [smem] + [vmem] * (count + len(terms) + 4),
        (shape((1, width, cols), bf16), shape((1, cols), f32), shape((1, rows), f32)),
        (anywhere, vmem, vmem),
        table_scratch(count, cols),
        count * rows * weight_block,
        count * weight_block,
    )(place, *[first[k] for k in range(count)], *terms, trans, gain, scale, info)
    return grad_weight, grad_bias, kl[0, :1]


def solution(mesh):
    placed = (
        P("section", None, "vocab"),
        P("section", "vocab"),
        P("section", None),
        P("section", None, "vocab"),
        P("section", "vocab"),
        P("vocab"),
        P("section", "vocab"),
    )
    return jax.shard_map(
        per_device,
        mesh=mesh,
        in_specs=placed,
        out_specs=(P("section", None, "vocab"), P("section", "vocab"), P("section")),
        check_vma=False,
    )
```

```python
import functools

import jax
import jax.numpy as jnp
from jax import lax
from jax.experimental import pallas as pl
from jax.experimental.pallas import tpu as pltpu
from jax.sharding import PartitionSpec as P

epsilon = 1e-05
f32 = jnp.float32
bf16 = jnp.bfloat16
words_height = 16
vmem = pl.BlockSpec(memory_space=pltpu.VMEM)
smem = pl.BlockSpec(memory_space=pltpu.SMEM)
main_memory = pl.BlockSpec(memory_space=pltpu.HBM)


def kernel_call(body, name, in_specs, out_shapes, out_specs, scratch, flops, moved):
    return pl.pallas_call(
        body,
        name=name,
        in_specs=in_specs,
        out_shape=out_shapes,
        out_specs=out_specs,
        scratch_shapes=scratch,
        cost_estimate=pl.CostEstimate(flops=flops, bytes_accessed=moved, transcendentals=0),
        compiler_params=pltpu.CompilerParams(vmem_limit_bytes=32 * 1024 * 1024),
    )


def in_main_memory(value):
    return pltpu.with_memory_space_constraint(value, pltpu.HBM)


def swap(value, offset, count):
    return lax.ppermute(value, "vocab", [(i, i ^ offset) for i in range(count)])


def after(value, *earlier):
    return lax.optimization_barrier((value, *earlier))[0]


def gather_pieces(own, count, also=()):
    pieces = {0: own}
    for k in range(4, count, 4):
        pieces[k] = swap(own, k, count)
    for number, base in enumerate(range(0, count, 4)):
        source = after(pieces[base], *also) if base else pieces[base]
        pieces[base + 1] = swap(source, 1, count)
        pieces[base + 2] = swap(source, 2, count)
        if number % 2:
            pieces[base + 3] = swap(pieces[base + 2], 1, count)
        else:
            pieces[base + 3] = swap(pieces[base + 1], 2, count)
    return pieces


def total(*parts):
    result = parts[0].astype(f32)
    for part in parts[1:]:
        result = result + part.astype(f32)
    return result


def scatter_sums(blocks, count):
    bases = list(range(0, count, 4))[::-1]
    far = {base: swap(blocks[base + 3], 1 if (base // 4) % 2 else 2, count) for base in bases}
    terms, near = [], {}
    for base in bases:
        x_part, y_part = blocks[base + 1], blocks[base + 2]
        if (base // 4) % 2:
            y_part = total(y_part, far[base]).astype(bf16)
        else:
            x_part = total(x_part, far[base]).astype(bf16)
        earlier = [far[base]] + near.get(base + 8, [])
        near[base] = [
            swap(after(x_part, *earlier), 1, count),
            swap(after(y_part, *earlier), 2, count),
        ]
        if base:
            terms.append(swap(total(blocks[base], *near[base]).astype(bf16), base, count))
        else:
            terms.extend((blocks[0], *near[base]))
    return terms


def pull(place, k, tables, buffer, sem):
    height = buffer.shape[0]
    index = place[0] ^ k
    if len(tables) == 1:
        rows = pl.ds(pl.multiple_of(index * height, height), height)
        pltpu.make_async_copy(tables[0].at[rows], buffer, sem).start()
        return
    per_table = tables[0].shape[0] // height
    rows = pl.ds(pl.multiple_of(lax.rem(index, per_table) * height, height), height)
    turn = lax.rem(lax.div(index, per_table) - place[1] + len(tables), len(tables))
    for number, table in enumerate(tables):

        @pl.when(turn == number)
        def _():
            pltpu.make_async_copy(table.at[rows], buffer, sem).start()


def arrived(tables, buffer, sem):
    pltpu.make_async_copy(tables[0].at[pl.ds(0, buffer.shape[0])], buffer, sem).wait()


def as_row(column):
    size = column.shape[0]
    return jnp.transpose(jnp.broadcast_to(column, (size, size)))[:1]


def as_column(row):
    size = row.shape[1]
    return jnp.transpose(jnp.broadcast_to(row, (size, size)))[:, :1]


def words_of(row, first):
    high = row.astype(bf16).astype(f32)
    middle = (row - high).astype(bf16).astype(f32)
    low = row - high - middle
    line = lax.broadcasted_iota(jnp.int32, (words_height, row.shape[1]), 0)
    block = jnp.where(line == first, high, 0.0)
    block = jnp.where(line == first + 1, middle, block)
    return jnp.where(line == first + 2, low, block)


def picked_rows(wanted, pool, offset):
    number = lax.broadcasted_iota(jnp.int32, (wanted.shape[0], pool.shape[0]), 1) + offset
    chosen = jnp.where(number == wanted, 1.0, 0.0).astype(bf16)
    return jnp.dot(chosen, pool, preferred_element_type=f32)


def inputs_kernel(wanted, pool, inputs):
    column = as_column(wanted[...].astype(f32)).astype(jnp.int32)
    inputs[...] = picked_rows(column, pool[0], 0).astype(bf16)


def head_kernel(place, wanted, inputs, gain, *refs):
    pools, (first, tail) = refs[:-2], refs[-2:]
    rows = inputs.shape[0]
    half = rows // 2
    height = pools[0].shape[0]
    count = height * len(pools)
    column = as_column(wanted[...].astype(f32)).astype(jnp.int32)
    turned = lax.rem(column - place[1] * height + count, count)
    value = sum(picked_rows(turned, pool[...], number * height) for number, pool in enumerate(pools))
    target = (value * gain[...].astype(f32)).astype(bf16)
    first[:rows] = inputs[...]
    first[rows:] = target[:half]
    tail[:half] = target[half:]
    tail[half:] = jnp.zeros((words_height, value.shape[1]), bf16)
    squares = as_row(jnp.sum(value * value, axis=1, keepdims=True))
    tail[half:, :rows] = words_of(squares, 3).astype(bf16)


def pull_all(place, order, tables, buffer, sems):
    for slot, k in enumerate(order):
        pull(place, k, tables, buffer.at[slot], sems.at[slot])


def early_trans_kernel(order, late, place, *refs):
    pieces, refs = refs[: len(order)], refs[len(order) :]
    weight, result, late_weight, buffer, sems, late_sems = refs
    rows = result.shape[0]
    pull_all(place, order, [weight], buffer, sems)
    pull_all(place, late, [weight], late_weight, late_sems)
    for slot in range(len(order)):
        arrived([weight], buffer.at[slot], sems.at[slot])
        part = jnp.dot(pieces[slot][:rows], buffer[slot], preferred_element_type=f32)
        if slot:
            result[...] += part
        else:
            result[...] = part
    for slot in range(len(late)):
        arrived([weight], late_weight.at[slot], late_sems.at[slot])


def late_trans_kernel(count, *refs):
    pieces, refs = refs[:count], refs[count:]
    weight, so_far, own, bias, gain, tail, trans, payload = refs
    rows = so_far.shape[0]
    trans[...] = so_far[...] + own[:rows].astype(f32) + bias[...].astype(f32)
    for slot in range(count):
        trans[...] += jnp.dot(pieces[slot][:rows], weight[slot], preferred_element_type=f32)
    value = trans[...]
    payload[:rows] = (value * gain[...].astype(f32)).astype(bf16)
    payload[rows:] = tail[...]
    squares = as_row(jnp.sum(value * value, axis=1, keepdims=True))
    start = payload.shape[0] - words_height
    payload[start:, :rows] = (
        words_of(squares, 0) + tail[-words_height:, :rows].astype(f32)
    ).astype(bf16)


def target_kernel(order, lines, table_count, place, *refs):
    pieces, refs = refs[: len(order)], refs[len(order) :]
    tables, refs = refs[:table_count], refs[table_count:]
    result, blocks, sems = refs
    pull_all(place, order, tables, blocks, sems)
    for slot in range(len(order)):
        arrived(tables, blocks.at[slot], sems.at[slot])
        part = jnp.dot(pieces[slot][lines[0] : lines[1]], blocks[slot], preferred_element_type=f32)
        if slot:
            result[...] += part
        else:
            result[...] = part


def early_logits_kernel(count, *refs):
    pieces, (blocks, result, word_sum) = refs[:count], refs[count:]
    for slot in range(count):
        part = jnp.dot(pieces[slot][...], blocks[slot], preferred_element_type=f32)
        if slot:
            result[...] += part
        else:
            result[...] = part
    word_sum[...] = sum(piece[-words_height:].astype(f32) for piece in pieces)


def late_logits_kernel(first, count, width, *refs):
    pieces, refs = refs[:count], refs[count:]
    blocks, so_far, early_words, target_half, logits, target_logits, stats, scale, acc = refs
    rows = logits.shape[0]
    half = target_half.shape[0]
    acc[...] = so_far[...]
    for slot in range(count):
        acc[...] += jnp.dot(pieces[slot][...], blocks[first + slot], preferred_element_type=f32)
    words = early_words[...] + sum(piece[-words_height:].astype(f32) for piece in pieces)
    words = words[:, :rows]
    trans_scale = lax.rsqrt((words[0:1] + words[1:2] + words[2:3]) / width + epsilon)
    final_scale = lax.rsqrt((words[3:4] + words[4:5] + words[5:6]) / width + epsilon)
    scale[...] = jnp.broadcast_to(trans_scale, scale.shape)
    trans_column, final_column = as_column(trans_scale), as_column(final_scale)
    trans_logits = acc[:rows] * trans_column
    logits[...] = trans_logits
    target_logits[:half] = target_half[...] * final_column[:half]
    target_logits[half:] = acc[rows : rows + rows - half] * final_column[half:]
    target = target_logits[...]
    trans_max = jnp.max(trans_logits, axis=1, keepdims=True)
    target_max = jnp.max(target, axis=1, keepdims=True)
    shifted = trans_logits - trans_max
    trans_exp = jnp.exp(shifted)
    target_exp = jnp.exp(target - target_max)
    columns = (
        trans_max,
        jnp.sum(trans_exp, axis=1, keepdims=True),
        jnp.sum(trans_exp * shifted, axis=1, keepdims=True),
        target_max,
        jnp.sum(target_exp, axis=1, keepdims=True),
        jnp.sum(target_exp * (target - trans_logits), axis=1, keepdims=True),
        jnp.sum(target_exp * shifted, axis=1, keepdims=True),
    )
    lane = lax.broadcasted_iota(jnp.int32, (rows, rows), 1)
    packed = jnp.zeros((rows, rows), f32)
    for number, column in enumerate(columns):
        packed = jnp.where(lane == number, column, packed)
    stats[...] = jnp.transpose(packed)[: stats.shape[0]]


def backward_block(dlogits, block):
    return lax.dot_general(
        dlogits, block, (((1,), (1,)), ((), ())), preferred_element_type=f32
    ).astype(bf16)


def first_backward_kernel(order, blocks, logits, target_logits, *refs):
    stats, (dlogits, info, *outs) = refs[:4], refs[4:]
    every = [part[i] for part in stats for i in range(part.shape[0])]
    top = functools.reduce(jnp.maximum, [s[0:1] for s in every])
    target_top = functools.reduce(jnp.maximum, [s[3:4] for s in every])
    trans_sum = target_sum = kl_sum = trans_dot = target_dot = 0.0
    for s in every:
        drop = s[0:1] - top
        factor = jnp.exp(drop)
        target_factor = jnp.exp(s[3:4] - target_top)
        trans_sum += factor * s[1:2]
        target_sum += target_factor * s[4:5]
        kl_sum += target_factor * s[5:6]
        trans_dot += factor * (s[2:3] + s[1:2] * drop)
        target_dot += target_factor * (s[6:7] + s[4:5] * drop)
    log_sum = top + jnp.log(trans_sum)
    target_log_sum = target_top + jnp.log(target_sum)
    value = (
        jnp.exp(logits[...] - as_column(log_sum))
        - jnp.exp(target_logits[...] - as_column(target_log_sum))
    ).astype(bf16)
    dlogits[...] = value
    line = lax.broadcasted_iota(jnp.int32, info.shape, 0)
    kl_rows = kl_sum / target_sum - (target_log_sum - log_sum)
    info[...] = jnp.where(line == 0, kl_rows, trans_dot / trans_sum - target_dot / target_sum)
    for k, out in zip(order, outs):
        out[...] = backward_block(value, blocks[k])


def later_backward_kernel(order, blocks, dlogits, *outs):
    value = dlogits[...]
    for k, out in zip(order, outs):
        out[...] = backward_block(value, blocks[k])


def weight_kernel(count, term_count, width, place, *refs):
    pieces, refs = refs[:count], refs[count:]
    terms, refs = refs[:term_count], refs[term_count:]
    trans, gain, scale, info, grad_weight, grad_bias, kl, buffer, sems = refs
    rows = trans.shape[0]
    height = buffer.shape[1]
    dnormed = functools.reduce(lambda a, b: a + b, [term[...].astype(f32) for term in terms])
    scale_row = scale[0:1]
    weight_row = scale_row * scale_row * info[1:2] / (width * scale_row)
    dtrans = as_column(scale_row) * (dnormed * gain[...].astype(f32) - trans[...] * as_column(weight_row))
    grad_bias[...] = jnp.sum(dtrans, axis=0, keepdims=True)
    kl[...] = jnp.broadcast_to(jnp.sum(info[0:1], axis=1, keepdims=True) / rows, kl.shape)
    rounded = dtrans.astype(bf16)
    copies = []
    for k in range(count):
        buffer[k] = lax.dot_general(
            pieces[k][:rows], rounded, (((0,), (0,)), ((), ())), preferred_element_type=f32
        ).astype(bf16)
        start = pl.multiple_of((place[0] ^ k) * height, height)
        copies.append(pltpu.make_async_copy(buffer.at[k], grad_weight.at[0, pl.ds(start, height)], sems.at[k]))
        copies[-1].start()
    for copy in copies:
        copy.wait()


def per_device(hidden, final_hidden, row_pick, trans_weight, trans_bias, norm_gain, unembed):
    count = lax.axis_size("vocab")
    sections = lax.axis_size("section")
    me = lax.axis_index("vocab")
    section = lax.axis_index("section")
    place = jnp.stack([me, section]).astype(jnp.int32)
    width, cols = trans_weight.shape[1:]
    rows = row_pick.shape[1]
    half = rows // 2
    weight = trans_weight[0]
    gain = norm_gain[None]
    shape = jax.ShapeDtypeStruct
    entries = unembed.shape[1]
    weight_block = 2 * cols * cols
    table_block = 2 * cols * entries

    def table_scratch(number, columns):
        return [pltpu.VMEM((number, cols, columns), bf16), pltpu.SemaphoreType.DMA((number,))]

    def from_others(value):
        return [
            lax.ppermute(value, "section", [((i + k) % sections, i) for i in range(sections)])
            for k in range(1, sections)
        ]

    final_pools = [final_hidden] + from_others(final_hidden)
    inputs = kernel_call(
        inputs_kernel,
        "inputs",
        [vmem] * 2,
        shape((rows, cols), bf16),
        vmem,
        [],
        0,
        hidden.shape[1] * cols * 2,
    )(row_pick, in_main_memory(hidden))
    first_own, tail = kernel_call(
        head_kernel,
        "head",
        [smem] + [vmem] * (3 + sections),
        (shape((rows + half, cols), bf16), shape((rows - half + words_height, cols), bf16)),
        (vmem, vmem),
        [],
        0,
        6 * rows * cols,
    )(place, row_pick, inputs, gain, *map(in_main_memory, final_pools))
    tables = [unembed] + from_others(after(unembed, first_own))
    first = gather_pieces(first_own, count, tables[1:])

    early = list(range(count // 2))
    late = list(range(count // 2, count))
    every = early + late
    side = len(early)
    so_far, late_weight = kernel_call(
        functools.partial(early_trans_kernel, early, late),
        "trans_early",
        [smem] + [vmem] * side + [main_memory],
        (shape((rows, cols), f32), shape((side, cols, cols), bf16)),
        (vmem, vmem),
        table_scratch(side, cols) + [pltpu.SemaphoreType.DMA((side,))],
        side * rows * weight_block,
        2 * side * weight_block,
    )(place, *[first[k] for k in early], in_main_memory(weight))
    payload_shape = shape((first_own.shape[0] + words_height, cols), bf16)
    trans, second_own = kernel_call(
        functools.partial(late_trans_kernel, side),
        "trans_late",
        [vmem] * (side + 6),
        (shape((rows, cols), f32), payload_shape),
        (vmem, vmem),
        [],
        side * rows * weight_block,
        side * weight_block,
    )(*[first[k] for k in late], late_weight, so_far, first_own, trans_bias, gain, tail)
    second = gather_pieces(second_own, count)

    target_half, blocks_in_order = kernel_call(
        functools.partial(target_kernel, every, (rows, rows + half), sections),
        "target_half",
        [smem] + [vmem] * count + [main_memory] * sections,
        (shape((half, entries), f32), shape((count, cols, entries), bf16)),
        (vmem, vmem),
        [pltpu.SemaphoreType.DMA((count,))],
        count * half * table_block,
        count * table_block,
    )(place, *[first[k] for k in every], *map(in_main_memory, tables))
    height = payload_shape.shape[0]
    so_far, words = kernel_call(
        functools.partial(early_logits_kernel, side),
        "logits_early",
        [vmem] * (side + 1),
        (shape((height, entries), f32), shape((words_height, cols), f32)),
        (vmem, vmem),
        [],
        side * height * table_block,
        side * table_block,
    )(*[second[k] for k in early], blocks_in_order)
    logits, target_logits, stats, scale = kernel_call(
        functools.partial(late_logits_kernel, side, side, width),
        "logits_late",
        [vmem] * (side + 4),
        (shape((rows, entries), f32), shape((rows, entries), f32), shape((8, rows), f32), shape((8, rows), f32)),
        (vmem,) * 4,
        [pltpu.VMEM((height, entries), f32)],
        side * height * table_block,
        side * table_block,
    )(*[second[k] for k in late], blocks_in_order, so_far, words, target_half)

    line_stats = jnp.stack([stats] + [swap(stats, k, count) for k in range(4, count, 4)])
    all_stats = [line_stats] + [swap(line_stats, k, count) for k in (1, 2, 3)]

    blocks = {}
    far = [base + 3 for base in range(0, count, 4)][::-1]
    piece = shape((rows, cols), bf16)
    dlogits, info, *made = kernel_call(
        functools.partial(first_backward_kernel, far),
        "backward_far",
        [vmem] * 7,
        (shape((rows, entries), bf16), shape((8, rows), f32), *[piece] * len(far)),
        (vmem,) * (2 + len(far)),
        [],
        len(far) * rows * table_block,
        len(far) * table_block,
    )(blocks_in_order, logits, target_logits, *all_stats)
    blocks.update(zip(far, made))
    bases = list(range(0, count, 4))[::-1]
    for number, part in enumerate((bases[: len(bases) // 2], bases[len(bases) // 2 :])):
        rest = [base + k for base in part for k in (1, 2, 0)]
        made = kernel_call(
            functools.partial(later_backward_kernel, rest),
            "backward_near_%d" % number,
            [vmem] * 2,
            tuple([piece] * len(rest)),
            (vmem,) * len(rest),
            [],
            len(rest) * rows * table_block,
            len(rest) * table_block,
        )(blocks_in_order, dlogits)
        blocks.update(zip(rest, made))
    terms = scatter_sums(blocks, count)

    grad_weight, grad_bias, kl = kernel_call(
        functools.partial(weight_kernel, count, len(terms), width),
        "grad_weight",
        [smem] + [vmem] * (count + len(terms) + 4),
        (shape((1, width, cols), bf16), shape((1, cols), f32), shape((1, rows), f32)),
        (main_memory, vmem, vmem),
        table_scratch(count, cols),
        count * rows * weight_block,
        count * weight_block,
    )(place, *[first[k] for k in range(count)], *terms, trans, gain, scale, info)
    return grad_weight, grad_bias, kl[0, :1]


def solution(mesh):
    placed = (
        P("section", None, "vocab"),
        P("section", "vocab"),
        P("section", None),
        P("section", None, "vocab"),
        P("section", "vocab"),
        P("vocab"),
        P("section", "vocab"),
    )
    return jax.shard_map(
        per_device,
        mesh=mesh,
        in_specs=placed,
        out_specs=(P("section", None, "vocab"), P("section", "vocab"), P("section")),
        check_vma=False,
    )
```

```python
import functools

import jax
import jax.numpy as jnp
from jax import lax
from jax.experimental import pallas as pl
from jax.experimental.pallas import tpu as pltpu
from jax.sharding import PartitionSpec as P

epsilon = 1e-05
f32 = jnp.float32
bf16 = jnp.bfloat16
words_height = 16
vmem = pl.BlockSpec(memory_space=pltpu.VMEM)
smem = pl.BlockSpec(memory_space=pltpu.SMEM)
anywhere = pl.BlockSpec(memory_space=pl.ANY)
main_memory = pl.BlockSpec(memory_space=pltpu.HBM)


def kernel_call(body, name, in_specs, out_shapes, out_specs, scratch, flops, moved):
    return pl.pallas_call(
        body,
        name=name,
        in_specs=in_specs,
        out_shape=out_shapes,
        out_specs=out_specs,
        scratch_shapes=scratch,
        cost_estimate=pl.CostEstimate(flops=flops, bytes_accessed=moved, transcendentals=0),
        compiler_params=pltpu.CompilerParams(vmem_limit_bytes=32 * 1024 * 1024),
    )


def in_main_memory(value):
    return pltpu.with_memory_space_constraint(value, pltpu.HBM)


def swap(value, offset, count):
    return lax.ppermute(value, "vocab", [(i, i ^ offset) for i in range(count)])


def after(value, *earlier):
    return lax.optimization_barrier((value, *earlier))[0]


def gather_pieces(own, count, before_last, make):
    pieces = {0: own}
    line = list(range(4, count, 4))
    for k in line[:-1]:
        pieces[k] = swap(own, k, count)
    pieces[line[-1]] = swap(after(own, *before_last) if before_last else own, line[-1], count)
    made = None
    for base in [0] + line:
        pieces[base + 1] = swap(pieces[base], 1, count)
        source = pieces[base]
        if make and base == line[len(line) // 2]:
            made = make()
            source = after(source, made)
        pieces[base + 2] = swap(source, 2, count)
        if (base // 4) % 2:
            pieces[base + 3] = swap(pieces[base + 2], 1, count)
        else:
            pieces[base + 3] = swap(pieces[base + 1], 2, count)
    return pieces, made


def total(*parts):
    result = parts[0].astype(f32)
    for part in parts[1:]:
        result = result + part.astype(f32)
    return result


def scatter_sums(blocks, count):
    bases = list(range(0, count, 4))[::-1]
    far, near, terms = {}, {}, []
    for base in bases:
        offset = 3 if base == bases[0] else 1 if (base // 4) % 2 else 2
        far[base] = swap(blocks[base + 3], offset, count)
    for base in bases:
        x_part, y_part = blocks[base + 1], blocks[base + 2]
        if base == bases[0]:
            near[base] = [far[base], swap(x_part, 1, count), swap(y_part, 2, count)]
        else:
            if (base // 4) % 2:
                y_part = total(y_part, far[base]).astype(bf16)
            else:
                x_part = total(x_part, far[base]).astype(bf16)
            earlier = near.get(base + 8, [])
            if earlier:
                x_part, y_part = after(x_part, *earlier), after(y_part, *earlier)
            near[base] = [swap(x_part, 1, count), swap(y_part, 2, count)]
        if base:
            terms.append(swap(total(blocks[base], *near[base]).astype(bf16), base, count))
        else:
            terms.extend((blocks[0], *near[base]))
    return terms


def pull(place, k, tables, buffer, sem):
    height = buffer.shape[0]
    index = place[0] ^ k
    if len(tables) == 1:
        rows = pl.ds(pl.multiple_of(index * height, height), height)
        pltpu.make_async_copy(tables[0].at[rows], buffer, sem).start()
        return
    per_table = tables[0].shape[0] // height
    rows = pl.ds(pl.multiple_of(lax.rem(index, per_table) * height, height), height)
    turn = lax.rem(lax.div(index, per_table) - place[1] + len(tables), len(tables))
    for number, table in enumerate(tables):

        @pl.when(turn == number)
        def _():
            pltpu.make_async_copy(table.at[rows], buffer, sem).start()


def arrived(tables, buffer, sem):
    pltpu.make_async_copy(tables[0].at[pl.ds(0, buffer.shape[0])], buffer, sem).wait()


def as_row(column):
    size = column.shape[0]
    return jnp.transpose(jnp.broadcast_to(column, (size, size)))[:1]


def as_column(row):
    size = row.shape[1]
    return jnp.transpose(jnp.broadcast_to(row, (size, size)))[:, :1]


def words_of(row, first):
    high = row.astype(bf16).astype(f32)
    middle = (row - high).astype(bf16).astype(f32)
    low = row - high - middle
    line = lax.broadcasted_iota(jnp.int32, (words_height, row.shape[1]), 0)
    block = jnp.where(line == first, high, 0.0)
    block = jnp.where(line == first + 1, middle, block)
    return jnp.where(line == first + 2, low, block)


def picked_rows(wanted, pool, offset):
    number = lax.broadcasted_iota(jnp.int32, (wanted.shape[0], pool.shape[0]), 1) + offset
    chosen = jnp.where(number == wanted, 1.0, 0.0).astype(bf16)
    return jnp.dot(chosen, pool, preferred_element_type=f32)


def inputs_kernel(wanted, pool, inputs):
    column = as_column(wanted[...].astype(f32)).astype(jnp.int32)
    inputs[...] = picked_rows(column, pool[0], 0).astype(bf16)


def target_kernel(place, wanted, gain, *refs):
    pools, tail = refs[:-1], refs[-1]
    height = pools[0].shape[0]
    count = height * len(pools)
    column = as_column(wanted[...].astype(f32)).astype(jnp.int32)
    rows = column.shape[0]
    turned = lax.rem(column - place[1] * height + count, count)
    value = sum(picked_rows(turned, pool[...], number * height) for number, pool in enumerate(pools))
    tail[:rows] = (value * gain[...].astype(f32).reshape(1, -1)).astype(bf16)
    tail[rows:] = jnp.zeros((words_height, value.shape[1]), bf16)
    squares = as_row(jnp.sum(value * value, axis=1, keepdims=True))
    tail[rows:, :rows] = words_of(squares, 3).astype(bf16)


def pull_all(place, order, tables, buffer, sems):
    for slot, k in enumerate(order):
        pull(place, k, tables, buffer.at[slot], sems.at[slot])


def fetch_kernel(order, table_count, place, *refs):
    tables, (blocks, sems) = refs[:table_count], refs[table_count:]
    pull_all(place, order, tables, blocks, sems)
    for slot in range(len(order)):
        arrived(tables, blocks.at[slot], sems.at[slot])


def add_products(result, pieces, lines, blocks, first):
    for slot, piece in enumerate(pieces):
        part = jnp.dot(piece[lines[0] : lines[1]], blocks[first + slot], preferred_element_type=f32)
        result[...] += part


def early_trans_kernel(count, *refs):
    pieces, (weight, own, bias, result) = refs[:count], refs[count:]
    rows = result.shape[0]
    result[...] = own[:rows].astype(f32) + bias[...].astype(f32)
    add_products(result, pieces, (0, rows), weight, 0)


def late_trans_kernel(count, *refs):
    pieces, refs = refs[:count], refs[count:]
    weight, so_far, gain, tail, trans, payload = refs
    rows = so_far.shape[0]
    trans[...] = so_far[...]
    add_products(trans, pieces, (0, rows), weight, count)
    value = trans[...]
    payload[:rows] = (value * gain[...].astype(f32).reshape(1, -1)).astype(bf16)
    payload[rows:] = tail[...]
    squares = as_row(jnp.sum(value * value, axis=1, keepdims=True))
    start = payload.shape[0] - words_height
    payload[start:, :rows] = (
        words_of(squares, 0) + tail[-words_height:, :rows].astype(f32)
    ).astype(bf16)


def early_logits_kernel(count, *refs):
    pieces, (blocks, result, word_sum) = refs[:count], refs[count:]
    result[...] = jnp.zeros(result.shape, f32)
    add_products(result, pieces, (0, result.shape[0]), blocks, 0)
    word_sum[...] = sum(piece[-words_height:].astype(f32) for piece in pieces)


def late_logits_kernel(first, count, width, *refs):
    pieces, refs = refs[:count], refs[count:]
    blocks, so_far, early_words, logits, target_logits, stats, scale, acc = refs
    rows = logits.shape[0]
    acc[...] = so_far[...]
    add_products(acc, pieces, (0, acc.shape[0]), blocks, first)
    words = early_words[...] + sum(piece[-words_height:].astype(f32) for piece in pieces)
    words = words[:, :rows]
    trans_scale = lax.rsqrt((words[0:1] + words[1:2] + words[2:3]) / width + epsilon)
    final_scale = lax.rsqrt((words[3:4] + words[4:5] + words[5:6]) / width + epsilon)
    scale[...] = jnp.broadcast_to(trans_scale, scale.shape)
    trans_column, final_column = as_column(trans_scale), as_column(final_scale)
    trans_logits = acc[:rows] * trans_column
    logits[...] = trans_logits
    target = acc[rows : 2 * rows] * final_column
    target_logits[...] = target
    trans_max = jnp.max(trans_logits, axis=1, keepdims=True)
    target_max = jnp.max(target, axis=1, keepdims=True)
    shifted = trans_logits - trans_max
    trans_exp = jnp.exp(shifted)
    target_exp = jnp.exp(target - target_max)
    columns = (
        trans_max,
        jnp.sum(trans_exp, axis=1, keepdims=True),
        jnp.sum(trans_exp * shifted, axis=1, keepdims=True),
        target_max,
        jnp.sum(target_exp, axis=1, keepdims=True),
        jnp.sum(target_exp * (target - trans_logits), axis=1, keepdims=True),
        jnp.sum(target_exp * shifted, axis=1, keepdims=True),
    )
    lane = lax.broadcasted_iota(jnp.int32, (rows, rows), 1)
    packed = jnp.zeros((rows, rows), f32)
    for number, column in enumerate(columns):
        packed = jnp.where(lane == number, column, packed)
    stats[...] = jnp.transpose(packed)[: stats.shape[0]]


def backward_block(dlogits, block):
    return lax.dot_general(
        dlogits, block, (((1,), (1,)), ((), ())), preferred_element_type=f32
    ).astype(bf16)


def first_backward_kernel(order, blocks, logits, target_logits, *refs):
    stats, (dlogits, info, *outs) = refs[:4], refs[4:]
    every = [part[i] for part in stats for i in range(part.shape[0])]
    top = functools.reduce(jnp.maximum, [s[0:1] for s in every])
    target_top = functools.reduce(jnp.maximum, [s[3:4] for s in every])
    trans_sum = target_sum = kl_sum = trans_dot = target_dot = 0.0
    for s in every:
        drop = s[0:1] - top
        factor = jnp.exp(drop)
        target_factor = jnp.exp(s[3:4] - target_top)
        trans_sum += factor * s[1:2]
        target_sum += target_factor * s[4:5]
        kl_sum += target_factor * s[5:6]
        trans_dot += factor * (s[2:3] + s[1:2] * drop)
        target_dot += target_factor * (s[6:7] + s[4:5] * drop)
    log_sum = top + jnp.log(trans_sum)
    target_log_sum = target_top + jnp.log(target_sum)
    value = (
        jnp.exp(logits[...] - as_column(log_sum))
        - jnp.exp(target_logits[...] - as_column(target_log_sum))
    ).astype(bf16)
    dlogits[...] = value
    line = lax.broadcasted_iota(jnp.int32, info.shape, 0)
    kl_rows = kl_sum / target_sum - (target_log_sum - log_sum)
    info[...] = jnp.where(line == 0, kl_rows, trans_dot / trans_sum - target_dot / target_sum)
    for k, out in zip(order, outs):
        out[...] = backward_block(value, blocks[k])


def later_backward_kernel(order, blocks, dlogits, *outs):
    value = dlogits[...]
    for k, out in zip(order, outs):
        out[...] = backward_block(value, blocks[k])


def weight_kernel(count, term_count, width, place, *refs):
    pieces, refs = refs[:count], refs[count:]
    terms, refs = refs[:term_count], refs[term_count:]
    trans, gain, scale, info, grad_weight, grad_bias, kl, buffer, sems = refs
    rows = trans.shape[0]
    height = buffer.shape[1]
    dnormed = functools.reduce(lambda a, b: a + b, [term[...].astype(f32) for term in terms])
    scale_row = scale[0:1]
    weight_row = scale_row * scale_row * info[1:2] / (width * scale_row)
    dtrans = as_column(scale_row) * (dnormed * gain[...].astype(f32).reshape(1, -1) - trans[...] * as_column(weight_row))
    grad_bias[...] = jnp.sum(dtrans, axis=0, keepdims=True)
    kl[...] = jnp.broadcast_to(jnp.sum(info[0:1], axis=1, keepdims=True) / rows, kl.shape)
    rounded = dtrans.astype(bf16)
    copies = []
    for k in range(count):
        buffer[k] = lax.dot_general(
            pieces[k][:rows], rounded, (((0,), (0,)), ((), ())), preferred_element_type=f32
        ).astype(bf16)
        start = pl.multiple_of((place[0] ^ k) * height, height)
        copies.append(pltpu.make_async_copy(buffer.at[k], grad_weight.at[0, pl.ds(start, height)], sems.at[k]))
        copies[-1].start()
    for copy in copies:
        copy.wait()


def per_device(hidden, final_hidden, row_pick, trans_weight, trans_bias, norm_gain, unembed):
    count = lax.axis_size("vocab")
    sections = lax.axis_size("section")
    me = lax.axis_index("vocab")
    section = lax.axis_index("section")
    place = jnp.stack([me, section]).astype(jnp.int32)
    width, cols = trans_weight.shape[1:]
    rows = row_pick.shape[1]
    weight = trans_weight[0]
    gain = norm_gain
    shape = jax.ShapeDtypeStruct
    entries = unembed.shape[1]
    weight_block = 2 * cols * cols
    table_block = 2 * cols * entries

    def table_scratch(number, columns):
        return [pltpu.VMEM((number, cols, columns), bf16), pltpu.SemaphoreType.DMA((number,))]

    def from_others(value):
        return [
            lax.ppermute(value, "section", [((i + k) % sections, i) for i in range(sections)])
            for k in range(1, sections)
        ]

    final_pools = [final_hidden] + from_others(final_hidden)
    first_own = kernel_call(
        inputs_kernel,
        "head",
        [vmem] * 2,
        shape((rows, cols), bf16),
        vmem,
        [],
        0,
        hidden.shape[1] * cols * 2,
    )(in_main_memory(row_pick), in_main_memory(hidden))
    tail = kernel_call(
        target_kernel,
        "target",
        [smem] + [vmem] * (2 + sections),
        shape((rows + words_height, cols), bf16),
        vmem,
        [],
        0,
        6 * rows * cols,
    )(place, in_main_memory(row_pick), gain, in_main_memory(final_hidden), *final_pools[1:])

    every = list(range(count))
    early, late = every[: count // 2], every[count // 2 :]
    side = len(early)

    def fetch(name, where, number_of_columns, *sources):
        return kernel_call(
            functools.partial(fetch_kernel, every, len(sources)),
            name,
            [smem, main_memory] + [anywhere] * (len(sources) - 1),
            shape((count, cols, number_of_columns), bf16),
            vmem,
            [pltpu.SemaphoreType.DMA((count,))],
            0,
            4 * count * cols * number_of_columns,
        )(where, in_main_memory(sources[0]), *sources[1:])

    tables = [unembed] + from_others(after(unembed, *final_pools[1:]))
    weight_blocks = fetch("weight_blocks", after(place, first_own), cols, weight)
    first, _ = gather_pieces(first_own, count, tables[1:], None)
    so_far = kernel_call(
        functools.partial(early_trans_kernel, side),
        "trans_early",
        [vmem] * (side + 3),
        shape((rows, cols), f32),
        vmem,
        [],
        side * rows * weight_block,
        side * weight_block,
    )(*[first[k] for k in early], weight_blocks, first_own, trans_bias)
    payload_shape = shape((rows + tail.shape[0], cols), bf16)
    trans, second_own = kernel_call(
        functools.partial(late_trans_kernel, side),
        "trans_late",
        [vmem] * (side + 4),
        (shape((rows, cols), f32), payload_shape),
        (vmem, vmem),
        [],
        side * rows * weight_block,
        side * weight_block,
    )(*[first[k] for k in late], weight_blocks, so_far, gain, tail)
    second, blocks_in_order = gather_pieces(
        second_own, count, (), lambda: fetch("unembed_blocks", after(place, second_own), entries, *tables)
    )

    height = payload_shape.shape[0]
    so_far, words = kernel_call(
        functools.partial(early_logits_kernel, side),
        "logits_early",
        [vmem] * (side + 1),
        (shape((height, entries), f32), shape((words_height, cols), f32)),
        (vmem, vmem),
        [],
        side * height * table_block,
        side * table_block,
    )(*[second[k] for k in early], blocks_in_order)
    logits, target_logits, stats, scale = kernel_call(
        functools.partial(late_logits_kernel, side, side, width),
        "logits_late",
        [vmem] * (side + 3),
        (shape((rows, entries), f32), shape((rows, entries), f32), shape((8, rows), f32), shape((8, rows), f32)),
        (vmem,) * 4,
        [pltpu.VMEM((height, entries), f32)],
        side * height * table_block,
        side * table_block,
    )(*[second[k] for k in late], blocks_in_order, so_far, words)

    line_stats = jnp.stack([stats] + [swap(stats, k, count) for k in range(4, count, 4)])
    all_stats = [line_stats] + [swap(line_stats, k, count) for k in (1, 2, 3)]

    blocks = {}
    last = count - 4
    far = [last + 3, last + 1, last + 2] + [base + 3 for base in range(0, last, 4)][::-1]
    piece = shape((rows, cols), bf16)
    dlogits, info, *made = kernel_call(
        functools.partial(first_backward_kernel, far),
        "backward_far",
        [vmem] * 7,
        (shape((rows, entries), bf16), shape((8, rows), f32), *[piece] * len(far)),
        (vmem,) * (2 + len(far)),
        [],
        len(far) * rows * table_block,
        len(far) * table_block,
    )(blocks_in_order, logits, target_logits, *all_stats)
    blocks.update(zip(far, made))
    bases = list(range(0, count, 4))[::-1]
    for number, part in enumerate((bases[: len(bases) // 2], bases[len(bases) // 2 :])):
        rest = [base + k for base in part for k in (1, 2, 0) if base + k not in far]
        made = kernel_call(
            functools.partial(later_backward_kernel, rest),
            "backward_near_%d" % number,
            [vmem] * 2,
            tuple([piece] * len(rest)),
            (vmem,) * len(rest),
            [],
            len(rest) * rows * table_block,
            len(rest) * table_block,
        )(blocks_in_order, dlogits)
        blocks.update(zip(rest, made))
    terms = scatter_sums(blocks, count)

    grad_weight, grad_bias, kl = kernel_call(
        functools.partial(weight_kernel, count, len(terms), width),
        "grad_weight",
        [smem] + [vmem] * (count + len(terms) + 4),
        (shape((1, width, cols), bf16), shape((1, cols), f32), shape((1, rows), f32)),
        (main_memory, vmem, vmem),
        table_scratch(count, cols),
        count * rows * weight_block,
        count * weight_block,
    )(place, *[first[k] for k in range(count)], *terms, trans, gain, scale, info)
    return grad_weight, grad_bias, kl[0, :1]


def solution(mesh):
    placed = (
        P("section", None, "vocab"),
        P("section", "vocab"),
        P("section", None),
        P("section", None, "vocab"),
        P("section", "vocab"),
        P("vocab"),
        P("section", "vocab"),
    )
    return jax.shard_map(
        per_device,
        mesh=mesh,
        in_specs=placed,
        out_specs=(P("section", None, "vocab"), P("section", "vocab"), P("section")),
        check_vma=False,
    )
```

```python
import functools

import jax
import jax.numpy as jnp
from jax import lax
from jax.experimental import pallas as pl
from jax.experimental.pallas import tpu as pltpu
from jax.sharding import PartitionSpec as P

epsilon = 1e-05
f32 = jnp.float32
bf16 = jnp.bfloat16
words_height = 8
vmem = pl.BlockSpec(memory_space=pltpu.VMEM)
smem = pl.BlockSpec(memory_space=pltpu.SMEM)
anywhere = pl.BlockSpec(memory_space=pl.ANY)
main_memory = pl.BlockSpec(memory_space=pltpu.HBM)


def kernel_call(body, name, in_specs, out_shapes, out_specs, scratch, flops, moved):
    return pl.pallas_call(
        body,
        name=name,
        in_specs=in_specs,
        out_shape=out_shapes,
        out_specs=out_specs,
        scratch_shapes=scratch,
        cost_estimate=pl.CostEstimate(flops=flops, bytes_accessed=moved, transcendentals=0),
        compiler_params=pltpu.CompilerParams(vmem_limit_bytes=32 * 1024 * 1024),
    )


def in_main_memory(value):
    return pltpu.with_memory_space_constraint(value, pltpu.HBM)


def swap(value, offset, count):
    return lax.ppermute(value, "vocab", [(i, i ^ offset) for i in range(count)])


def after(value, *earlier):
    return lax.optimization_barrier((value, *earlier))[0]


def gather_pieces(own, count, before_last, make):
    pieces = {0: own}
    line = list(range(4, count, 4))
    for k in line[:-1]:
        pieces[k] = swap(own, k, count)
    pieces[line[-1]] = swap(after(own, *before_last) if before_last else own, line[-1], count)
    made = None
    for base in [0] + line:
        pieces[base + 1] = swap(pieces[base], 1, count)
        source = pieces[base]
        if make and base == line[len(line) // 2]:
            made = make()
            source = after(source, made)
        pieces[base + 2] = swap(source, 2, count)
        if (base // 4) % 2:
            pieces[base + 3] = swap(pieces[base + 2], 1, count)
        else:
            pieces[base + 3] = swap(pieces[base + 1], 2, count)
    return pieces, made


def total(*parts):
    result = parts[0].astype(f32)
    for part in parts[1:]:
        result = result + part.astype(f32)
    return result


def scatter_sums(blocks, count):
    bases = list(range(0, count, 4))[::-1]
    far, near, terms = {}, {}, []
    for base in bases:
        offset = 3 if base == bases[0] else 1 if (base // 4) % 2 else 2
        far[base] = swap(blocks[base + 3], offset, count)
    for base in bases:
        x_part, y_part = blocks[base + 1], blocks[base + 2]
        if base == bases[0]:
            near[base] = [far[base], swap(x_part, 1, count), swap(y_part, 2, count)]
        else:
            if (base // 4) % 2:
                y_part = total(y_part, far[base]).astype(bf16)
            else:
                x_part = total(x_part, far[base]).astype(bf16)
            earlier = near.get(base + 8, [])
            if earlier:
                x_part, y_part = after(x_part, *earlier), after(y_part, *earlier)
            near[base] = [swap(x_part, 1, count), swap(y_part, 2, count)]
        if base:
            terms.append(swap(total(blocks[base], *near[base]).astype(bf16), base, count))
        else:
            terms.extend((blocks[0], *near[base]))
    return terms


def pull(place, k, tables, buffer, sem):
    height = buffer.shape[0]
    index = place[0] ^ k
    if len(tables) == 1:
        rows = pl.ds(pl.multiple_of(index * height, height), height)
        pltpu.make_async_copy(tables[0].at[rows], buffer, sem).start()
        return
    per_table = tables[0].shape[0] // height
    rows = pl.ds(pl.multiple_of(lax.rem(index, per_table) * height, height), height)
    turn = lax.rem(lax.div(index, per_table) - place[1] + len(tables), len(tables))
    for number, table in enumerate(tables):

        @pl.when(turn == number)
        def _():
            pltpu.make_async_copy(table.at[rows], buffer, sem).start()


def arrived(tables, buffer, sem):
    pltpu.make_async_copy(tables[0].at[pl.ds(0, buffer.shape[0])], buffer, sem).wait()


def as_row(column):
    size = column.shape[0]
    return jnp.transpose(jnp.broadcast_to(column, (size, size)))[:1]


def as_column(row):
    size = row.shape[1]
    return jnp.transpose(jnp.broadcast_to(row, (size, size)))[:, :1]


def words_of(row, first):
    high = row.astype(bf16).astype(f32)
    middle = (row - high).astype(bf16).astype(f32)
    low = row - high - middle
    line = lax.broadcasted_iota(jnp.int32, (words_height, row.shape[1]), 0)
    block = jnp.where(line == first, high, 0.0)
    block = jnp.where(line == first + 1, middle, block)
    return jnp.where(line == first + 2, low, block)


def picked_rows(wanted, pool, offset):
    number = lax.broadcasted_iota(jnp.int32, (wanted.shape[0], pool.shape[0]), 1) + offset
    chosen = jnp.where(number == wanted, 1.0, 0.0).astype(bf16)
    return jnp.dot(chosen, pool, preferred_element_type=f32)


def inputs_kernel(wanted, pool, inputs):
    column = as_column(wanted[...].astype(f32)).astype(jnp.int32)
    inputs[...] = picked_rows(column, pool[0], 0).astype(bf16)


def target_kernel(place, wanted, gain, *refs):
    pools, tail = refs[:-1], refs[-1]
    height = pools[0].shape[0]
    count = height * len(pools)
    column = as_column(wanted[...].astype(f32)).astype(jnp.int32)
    rows = column.shape[0]
    turned = lax.rem(column - place[1] * height + count, count)
    value = sum(picked_rows(turned, pool[...], number * height) for number, pool in enumerate(pools))
    tail[:rows] = (value * gain[...].astype(f32).reshape(1, -1)).astype(bf16)
    tail[rows:] = jnp.zeros((words_height, value.shape[1]), bf16)
    squares = as_row(jnp.sum(value * value, axis=1, keepdims=True))
    tail[rows:, :rows] = words_of(squares, 3).astype(bf16)


def pull_all(place, order, tables, buffer, sems):
    for slot, k in enumerate(order):
        pull(place, k, tables, buffer.at[slot], sems.at[slot])


def fetch_kernel(order, table_count, place, *refs):
    tables, (blocks, sems) = refs[:table_count], refs[table_count:]
    pull_all(place, order, tables, blocks, sems)
    for slot in range(len(order)):
        arrived(tables, blocks.at[slot], sems.at[slot])


def add_products(result, pieces, lines, blocks, first):
    for slot, piece in enumerate(pieces):
        part = jnp.dot(piece[lines[0] : lines[1]], blocks[first + slot], preferred_element_type=f32)
        result[...] += part


def early_trans_kernel(count, *refs):
    pieces, (weight, own, bias, result) = refs[:count], refs[count:]
    rows = result.shape[0]
    result[...] = own[:rows].astype(f32) + bias[...].astype(f32)
    add_products(result, pieces, (0, rows), weight, 0)


def late_trans_kernel(count, *refs):
    pieces, refs = refs[:count], refs[count:]
    weight, so_far, gain, tail, trans, payload = refs
    rows = so_far.shape[0]
    trans[...] = so_far[...]
    add_products(trans, pieces, (0, rows), weight, count)
    value = trans[...]
    payload[:rows] = (value * gain[...].astype(f32).reshape(1, -1)).astype(bf16)
    payload[rows:] = tail[...]
    squares = as_row(jnp.sum(value * value, axis=1, keepdims=True))
    start = payload.shape[0] - words_height
    payload[start:, :rows] = (
        words_of(squares, 0) + tail[-words_height:, :rows].astype(f32)
    ).astype(bf16)


def early_logits_kernel(count, *refs):
    pieces, (blocks, result, word_sum) = refs[:count], refs[count:]
    result[...] = jnp.zeros(result.shape, f32)
    add_products(result, pieces, (0, result.shape[0]), blocks, 0)
    word_sum[...] = sum(piece[-words_height:].astype(f32) for piece in pieces)


def late_logits_kernel(first, count, width, *refs):
    pieces, refs = refs[:count], refs[count:]
    blocks, so_far, early_words, logits, target_logits, stats, scale, acc = refs
    rows = logits.shape[0]
    acc[...] = so_far[...]
    add_products(acc, pieces, (0, acc.shape[0]), blocks, first)
    words = early_words[...] + sum(piece[-words_height:].astype(f32) for piece in pieces)
    words = words[:, :rows]
    trans_scale = lax.rsqrt((words[0:1] + words[1:2] + words[2:3]) / width + epsilon)
    final_scale = lax.rsqrt((words[3:4] + words[4:5] + words[5:6]) / width + epsilon)
    scale[...] = jnp.broadcast_to(trans_scale, scale.shape)
    trans_column, final_column = as_column(trans_scale), as_column(final_scale)
    trans_logits = acc[:rows] * trans_column
    logits[...] = trans_logits
    target = acc[rows : 2 * rows] * final_column
    target_logits[...] = target
    trans_max = jnp.max(trans_logits, axis=1, keepdims=True)
    target_max = jnp.max(target, axis=1, keepdims=True)
    shifted = trans_logits - trans_max
    trans_exp = jnp.exp(shifted)
    target_exp = jnp.exp(target - target_max)
    columns = (
        trans_max,
        jnp.sum(trans_exp, axis=1, keepdims=True),
        jnp.sum(trans_exp * shifted, axis=1, keepdims=True),
        target_max,
        jnp.sum(target_exp, axis=1, keepdims=True),
        jnp.sum(target_exp * (target - trans_logits), axis=1, keepdims=True),
        jnp.sum(target_exp * shifted, axis=1, keepdims=True),
    )
    lane = lax.broadcasted_iota(jnp.int32, (rows, rows), 1)
    packed = jnp.zeros((rows, rows), f32)
    for number, column in enumerate(columns):
        packed = jnp.where(lane == number, column, packed)
    stats[...] = jnp.transpose(packed)[: stats.shape[0]]


def backward_block(dlogits, block):
    return lax.dot_general(
        dlogits, block, (((1,), (1,)), ((), ())), preferred_element_type=f32
    ).astype(bf16)


def first_backward_kernel(order, blocks, logits, target_logits, *refs):
    stats, (dlogits, info, *outs) = refs[:4], refs[4:]
    every = [part[i] for part in stats for i in range(part.shape[0])]
    top = functools.reduce(jnp.maximum, [s[0:1] for s in every])
    target_top = functools.reduce(jnp.maximum, [s[3:4] for s in every])
    trans_sum = target_sum = kl_sum = trans_dot = target_dot = 0.0
    for s in every:
        drop = s[0:1] - top
        factor = jnp.exp(drop)
        target_factor = jnp.exp(s[3:4] - target_top)
        trans_sum += factor * s[1:2]
        target_sum += target_factor * s[4:5]
        kl_sum += target_factor * s[5:6]
        trans_dot += factor * (s[2:3] + s[1:2] * drop)
        target_dot += target_factor * (s[6:7] + s[4:5] * drop)
    log_sum = top + jnp.log(trans_sum)
    target_log_sum = target_top + jnp.log(target_sum)
    value = (
        jnp.exp(logits[...] - as_column(log_sum))
        - jnp.exp(target_logits[...] - as_column(target_log_sum))
    ).astype(bf16)
    dlogits[...] = value
    line = lax.broadcasted_iota(jnp.int32, info.shape, 0)
    kl_rows = kl_sum / target_sum - (target_log_sum - log_sum)
    info[...] = jnp.where(line == 0, kl_rows, trans_dot / trans_sum - target_dot / target_sum)
    for k, out in zip(order, outs):
        out[...] = backward_block(value, blocks[k])


def later_backward_kernel(order, blocks, dlogits, *outs):
    value = dlogits[...]
    for k, out in zip(order, outs):
        out[...] = backward_block(value, blocks[k])


def last_backward_kernel(order, width, blocks, dlogits, trans, gain, scale, info, factor, offset, *outs):
    later_backward_kernel(order, blocks, dlogits, *outs)
    scale_row = scale[0:1]
    factor[...] = as_column(scale_row) * gain[...].astype(f32).reshape(1, -1)
    offset[...] = trans[...] * as_column(scale_row * scale_row * info[1:2] / width)


def weight_kernel(count, term_count, place, *refs):
    pieces, refs = refs[:count], refs[count:]
    terms, refs = refs[:term_count], refs[term_count:]
    factor, offset, info, grad_weight, grad_bias, kl, buffer, sems, bias_sum, kl_sum, small_sems = refs
    rows = factor.shape[0]
    height = buffer.shape[1]
    dnormed = functools.reduce(lambda a, b: a + b, [term[...].astype(f32) for term in terms])
    dtrans = dnormed * factor[...] - offset[...]
    rounded = dtrans.astype(bf16)
    bias_sum[...] = jnp.sum(dtrans, axis=0, keepdims=True)
    kl_sum[...] = jnp.broadcast_to(jnp.sum(info[0:1], axis=1, keepdims=True) / rows, kl_sum.shape)
    copies = [
        pltpu.make_async_copy(bias_sum, grad_bias, small_sems.at[0]),
        pltpu.make_async_copy(kl_sum, kl, small_sems.at[1]),
    ]
    for copy in copies:
        copy.start()
    for k in range(count):
        buffer[k] = lax.dot_general(
            pieces[k][:rows], rounded, (((0,), (0,)), ((), ())), preferred_element_type=f32
        ).astype(bf16)
        start = pl.multiple_of((place[0] ^ k) * height, height)
        copies.append(pltpu.make_async_copy(buffer.at[k], grad_weight.at[0, pl.ds(start, height)], sems.at[k]))
        copies[-1].start()
    for copy in copies:
        copy.wait()


def per_device(hidden, final_hidden, row_pick, trans_weight, trans_bias, norm_gain, unembed):
    count = lax.axis_size("vocab")
    sections = lax.axis_size("section")
    me = lax.axis_index("vocab")
    section = lax.axis_index("section")
    place = jnp.stack([me, section]).astype(jnp.int32)
    width, cols = trans_weight.shape[1:]
    rows = row_pick.shape[1]
    weight = trans_weight[0]
    gain = norm_gain
    shape = jax.ShapeDtypeStruct
    entries = unembed.shape[1]
    weight_block = 2 * cols * cols
    table_block = 2 * cols * entries

    def table_scratch(number, columns):
        return [pltpu.VMEM((number, cols, columns), bf16), pltpu.SemaphoreType.DMA((number,))]

    def from_others(value):
        return [
            lax.ppermute(value, "section", [((i + k) % sections, i) for i in range(sections)])
            for k in range(1, sections)
        ]

    final_pools = [final_hidden] + from_others(final_hidden)
    first_own = kernel_call(
        inputs_kernel,
        "head",
        [vmem] * 2,
        shape((rows, cols), bf16),
        vmem,
        [],
        0,
        hidden.shape[1] * cols * 2,
    )(in_main_memory(row_pick), in_main_memory(hidden))
    def make_tail():
        return kernel_call(
            target_kernel,
            "target",
            [smem] + [vmem] * (2 + sections),
            shape((rows + words_height, cols), bf16),
            vmem,
            [],
            0,
            6 * rows * cols,
        )(place, in_main_memory(row_pick), gain, in_main_memory(final_hidden), *final_pools[1:])

    every = list(range(count))
    early, late = every[: count // 2], every[count // 2 :]
    side = len(early)

    def fetch(name, where, number_of_columns, *sources):
        return kernel_call(
            functools.partial(fetch_kernel, every, len(sources)),
            name,
            [smem, main_memory] + [anywhere] * (len(sources) - 1),
            shape((count, cols, number_of_columns), bf16),
            vmem,
            [pltpu.SemaphoreType.DMA((count,))],
            0,
            4 * count * cols * number_of_columns,
        )(where, in_main_memory(sources[0]), *sources[1:])

    tables = [unembed] + from_others(after(unembed, *final_pools[1:]))
    weight_blocks = fetch("weight_blocks", after(place, first_own), cols, weight)
    first, tail = gather_pieces(first_own, count, tables[1:], make_tail)
    so_far = kernel_call(
        functools.partial(early_trans_kernel, side),
        "trans_early",
        [vmem] * (side + 3),
        shape((rows, cols), f32),
        vmem,
        [],
        side * rows * weight_block,
        side * weight_block,
    )(*[first[k] for k in early], weight_blocks, first_own, trans_bias)
    payload_shape = shape((rows + tail.shape[0], cols), bf16)
    trans, second_own = kernel_call(
        functools.partial(late_trans_kernel, side),
        "trans_late",
        [vmem] * (side + 4),
        (shape((rows, cols), f32), payload_shape),
        (vmem, vmem),
        [],
        side * rows * weight_block,
        side * weight_block,
    )(*[first[k] for k in late], weight_blocks, so_far, gain, tail)
    second, blocks_in_order = gather_pieces(
        second_own, count, (), lambda: fetch("unembed_blocks", after(place, second_own), entries, *tables)
    )

    height = payload_shape.shape[0]
    so_far, words = kernel_call(
        functools.partial(early_logits_kernel, side),
        "logits_early",
        [vmem] * (side + 1),
        (shape((height, entries), f32), shape((words_height, cols), f32)),
        (vmem, vmem),
        [],
        side * height * table_block,
        side * table_block,
    )(*[second[k] for k in early], blocks_in_order)
    logits, target_logits, stats, scale = kernel_call(
        functools.partial(late_logits_kernel, side, side, width),
        "logits_late",
        [vmem] * (side + 3),
        (shape((rows, entries), f32), shape((rows, entries), f32), shape((8, rows), f32), shape((8, rows), f32)),
        (vmem,) * 4,
        [pltpu.VMEM((height, entries), f32)],
        side * height * table_block,
        side * table_block,
    )(*[second[k] for k in late], blocks_in_order, so_far, words)

    line_stats = jnp.stack([stats] + [swap(stats, k, count) for k in range(4, count, 4)])
    all_stats = [line_stats] + [swap(line_stats, k, count) for k in (1, 2, 3)]

    blocks = {}
    last = count - 4
    far = [last + 3, last + 1, last + 2] + [base + 3 for base in range(0, last, 4)][::-1]
    piece = shape((rows, cols), bf16)
    dlogits, info, *made = kernel_call(
        functools.partial(first_backward_kernel, far),
        "backward_far",
        [vmem] * 7,
        (shape((rows, entries), bf16), shape((8, rows), f32), *[piece] * len(far)),
        (vmem,) * (2 + len(far)),
        [],
        len(far) * rows * table_block,
        len(far) * table_block,
    )(blocks_in_order, logits, target_logits, *all_stats)
    blocks.update(zip(far, made))
    bases = list(range(0, count, 4))[::-1]
    halves = bases[: len(bases) // 2], bases[len(bases) // 2 :]
    rests = [[base + k for base in part for k in (1, 2, 0) if base + k not in far] for part in halves]
    made = kernel_call(
        functools.partial(later_backward_kernel, rests[0]),
        "backward_near_0",
        [vmem] * 2,
        tuple([piece] * len(rests[0])),
        (vmem,) * len(rests[0]),
        [],
        len(rests[0]) * rows * table_block,
        len(rests[0]) * table_block,
    )(blocks_in_order, dlogits)
    blocks.update(zip(rests[0], made))
    factor, offset, *made = kernel_call(
        functools.partial(last_backward_kernel, rests[1], width),
        "backward_near_1",
        [vmem] * 6,
        (shape((rows, cols), f32),) * 2 + (piece,) * len(rests[1]),
        (vmem,) * (2 + len(rests[1])),
        [],
        len(rests[1]) * rows * table_block,
        len(rests[1]) * table_block,
    )(blocks_in_order, dlogits, trans, gain, scale, info)
    blocks.update(zip(rests[1], made))
    terms = scatter_sums(blocks, count)

    grad_weight, grad_bias, kl = kernel_call(
        functools.partial(weight_kernel, count, len(terms)),
        "grad_weight",
        [smem] + [vmem] * (count + len(terms) + 3),
        (shape((1, width, cols), bf16), shape((1, cols), f32), shape((1, rows), f32)),
        (main_memory,) * 3,
        table_scratch(count, cols)
        + [pltpu.VMEM((1, cols), f32), pltpu.VMEM((1, rows), f32), pltpu.SemaphoreType.DMA((2,))],
        count * rows * weight_block,
        count * weight_block,
    )(place, *[first[k] for k in range(count)], *terms, factor, offset, info)
    return grad_weight, grad_bias, kl[0, :1]


def solution(mesh):
    placed = (
        P("section", None, "vocab"),
        P("section", "vocab"),
        P("section", None),
        P("section", None, "vocab"),
        P("section", "vocab"),
        P("vocab"),
        P("section", "vocab"),
    )
    return jax.shard_map(
        per_device,
        mesh=mesh,
        in_specs=placed,
        out_specs=(P("section", None, "vocab"), P("section", "vocab"), P("section")),
        check_vma=False,
    )
```
